32 devices in a mesh: section: 4 (over y, x), resp: 8 (over z, core).
Axes of the slice: x: 2, y: 2, z: 4, core: 2. Of those that a mesh axis runs over, the one named last changes fastest.
Arguments:
- queries: bfloat16 [4, 512, 4096], P('section', 'resp'), may hold values from -100 to 100
- resp_kv: bfloat16 [4, 512, 1024], P('section', 'resp'), may hold values from -4 to 4
- prefix_kv: bfloat16 [4, 4096, 1024], P('section', 'resp'), may hold values from -6 to 6
- owner: int32 [4, 4], P('section'), may hold values from 0 to 7, as said below
- seg_len: int32 [16, 4], P('resp'), may hold values from 1 to 16, 32 in all within a row
Outputs:
- out: bfloat16 [4, 512, 4096], P('section', 'resp')
The draws below stay inside these ranges and needn't reach their ends.
Inputs may be any that keep to these rules, and one draw needn't show every extreme that they name: owner[l, p] is one of the devices p * 2 to (p + 1) * 2 - 1, those holding prompt p's responses.
All inputs are finite; a program needn't handle non-finite values.
Results may differ from the reference program's by a relative error of at most 0.0099.
Values may be sent and summed in bfloat16 or wider, within the bound.
A program may use at most 64 MiB of HBM per device.

```python
import math
import jax
import jax.numpy as jnp
import numpy as np
from jax import lax

HQ = 32
KVH = 4
HEAD_SIZE = 128
PLEN = 512
TOKM = 32
MB = 2
RESPS = 4
PROMPTS = 4
KVW = 512
MOSTLEN = 16
LAYERS = 4
ROWS = 512
N_RESP = 8


def common_parts(key):
    group_size = N_RESP // PROMPTS
    owner_ranks = jax.random.randint(jax.random.fold_in(key, 11), (LAYERS, PROMPTS), 0, group_size)
    owner_ranks = owner_ranks.at[0, 0].set(0).at[LAYERS - 1, PROMPTS - 1].set(group_size - 1)
    owners = owner_ranks + (jnp.arange(PROMPTS, dtype=jnp.int32) * group_size)[None, :]
    key_table = jnp.clip(jax.random.normal(jax.random.fold_in(key, 13), (LAYERS, N_RESP * PLEN, KVH * HEAD_SIZE), jnp.float32), -4.0, 4.0)
    return (owners.astype(jnp.int32), key_table)


def draw_owner(key, part):
    owners, key_table = common_parts(key)
    return owners


def draw_prefix_kv(key, part):
    owners, key_table = common_parts(key)
    key = jax.random.fold_in(key, 3)
    value_shape = (LAYERS, N_RESP * PLEN, KVH * HEAD_SIZE)
    values = jnp.clip(jax.random.normal(jax.random.fold_in(key, 2), value_shape, jnp.float32), -4.0, 4.0)
    return jnp.concatenate([key_table, values], axis=2).astype(jnp.bfloat16)


def draw_queries(key, part):
    key = jax.random.fold_in(key, 5)
    full_shape = (LAYERS, ROWS, HQ * HEAD_SIZE)
    return jnp.clip(jax.random.normal(key, full_shape, jnp.float32), -4.0, 4.0).astype(jnp.bfloat16)


def steps_of(stream_key, extent, cuts, least, largest):
    level, own = 1.0, jax.random.fold_in(stream_key, 6)
    for dim, shards_of in cuts:
        heights = jnp.exp(jax.random.uniform(jax.random.fold_in(own, dim), (shards_of,), jnp.float32, least / len(cuts), largest / len(cuts)))
        level = level * jnp.repeat(heights, extent[dim] // shards_of).reshape([-1 if axis == dim else 1 for axis in range(len(extent))])
    return level


def profile(number_of, total, most, slope):
    weights = [(1 << 20) // math.isqrt(grade ** slope) + 1 for grade in range(2, number_of + 1)]
    spare, holding = total - most - (number_of - 1), [1] * (number_of - 1)
    while spare > 0:
        candidates = [i for i in range(number_of - 1) if holding[i] < most]
        mass, remaining = sum([weights[i] for i in candidates]), spare
        for i in candidates:
            extra = min(most - holding[i], max(1, remaining * weights[i] // mass), spare)
            holding[i] = holding[i] + extra
            spare = spare - extra
    return np.array([most] + holding)


def uneven_parts(stream_key, count, total, bound, slope):
    if count == 2:
        one = jax.random.randint(stream_key, (), max(1, total - bound), min(bound, total - 1) + 1)
        return jnp.stack([one, total - one])
    sizes = jnp.asarray(profile(count, total, bound, slope), jnp.int32)
    couples = (count - 1) // 2
    giver, sink = sizes[1:1 + 2 * couples:2], sizes[2:2 + 2 * couples:2]
    slack = jnp.minimum(giver - 1, bound - sink)
    moved = jax.random.randint(jax.random.fold_in(stream_key, 1), (couples,), 0, 1 << 20) % (slack + 1)
    sizes = sizes.at[1:1 + 2 * couples:2].set(giver - moved).at[2:2 + 2 * couples:2].set(sink + moved)
    return sizes[jax.random.permutation(jax.random.fold_in(stream_key, 2), count)]


def normal_values(key, dims, scale, bound, pieces=(), kind=jnp.bfloat16):
    loudness = steps_of(key, dims, pieces, -0.22, 0.18) if pieces else 1.0
    drawn = jax.random.normal(key, dims, jnp.float32) * scale * loudness
    return jnp.minimum(jnp.maximum(drawn, -bound), bound).astype(kind)


def setup_inputs(seed: int = 0) -> dict:
    key_list = jax.random.split(jax.random.key(seed), 6)
    return {
        "queries": draw_queries(jax.random.fold_in(key_list[5], 71), 0),
        "resp_kv": normal_values(key_list[1], (LAYERS, ROWS, 2 * KVW), 1.0, 4.0, ((0, 4), (1, 8))),
        "prefix_kv": draw_prefix_kv(jax.random.fold_in(key_list[5], 71), 0),
        "owner": draw_owner(jax.random.fold_in(key_list[5], 71), 0),
        "seg_len": jax.vmap(lambda own: uneven_parts(own, RESPS, TOKM, MOSTLEN, 2))(jax.random.split(key_list[4], (N_RESP * MB))).reshape((N_RESP * MB, RESPS)).astype(jnp.int32),
    }


EPS = 1e-06

def same_response(lengths, count_of_rows):
    ends = jnp.cumsum(lengths).astype(jnp.int32)
    position = jnp.arange(count_of_rows, dtype=jnp.int32)
    response = lax.optimization_barrier(jnp.sum((position[:, None] >= ends[None, :]).astype(jnp.int32), axis=1)).astype(jnp.int32)
    return (response[:, None] == response[None, :]) & (position[None, :] <= position[:, None])

def attend(mixed, prefix, local_rows, local_lengths):
    count_of_rows = mixed.shape[0]
    kv_width = prefix.shape[1] // 2
    groups = kv_width // HEAD_SIZE
    joined = jnp.concatenate([prefix, local_rows], axis=0)
    key_matrix = joined[:, :kv_width].reshape(-1, groups, HEAD_SIZE).astype(jnp.float32)
    value_matrix = joined[:, kv_width:].reshape(-1, groups, HEAD_SIZE).astype(jnp.float32)
    heads_of_query = mixed.reshape(count_of_rows, groups, HQ // groups, HEAD_SIZE).astype(jnp.float32)
    logit_scores = jnp.einsum('fiqv,civ->iqfc', heads_of_query, key_matrix) * (1.0 / math.sqrt(HEAD_SIZE))
    allowed = jnp.concatenate([jnp.ones((count_of_rows, prefix.shape[0]), bool), same_response(local_lengths, count_of_rows)], axis=1)
    logit_scores = jnp.where(allowed[None, None], logit_scores, -jnp.inf)
    row_top = lax.optimization_barrier(jnp.max(logit_scores, axis=3, keepdims=True))
    expo = jnp.exp(logit_scores - row_top)
    softmax_weights = (expo / lax.optimization_barrier(jnp.sum(expo, axis=3, keepdims=True))).astype(jnp.bfloat16)
    attended_output = jnp.einsum('euzm,meh->zeuh', softmax_weights.astype(jnp.float32), value_matrix).reshape(count_of_rows, -1)
    square = lax.optimization_barrier(jnp.mean(attended_output * attended_output, axis=1, keepdims=True))
    return (attended_output * lax.rsqrt(square + EPS)).astype(jnp.bfloat16)

def reference(queries, resp_kv, prefix_kv, owner, seg_len):
    group_size = N_RESP // PROMPTS
    lengths = seg_len.reshape(N_RESP, MB, RESPS)
    carried = jnp.zeros((N_RESP, MB, TOKM, HQ * HEAD_SIZE), jnp.bfloat16)
    outputs = []
    for layer_index in range(LAYERS):
        layer_queries = queries[layer_index].reshape(N_RESP, MB, TOKM, -1)
        layer_local = resp_kv[layer_index].reshape(N_RESP, MB, TOKM, -1)
        prefix_slots = prefix_kv[layer_index].reshape(N_RESP, PLEN, -1)
        owner_row = owner[layer_index]

        def per_device(packed_args):
            device_index, query_dev, local_dev, carry_dev, length_dev = packed_args
            root_owner = owner_row[device_index // group_size].astype(jnp.int32)
            prefix = lax.dynamic_index_in_dim(prefix_slots, root_owner, 0, keepdims=False)

            def per_micro(inner_args):
                query_rows, local_rows, carry_rows, local_lengths = inner_args
                mixed = (query_rows.astype(jnp.float32) + carry_rows.astype(jnp.float32)).astype(jnp.bfloat16)
                return attend(mixed, prefix, local_rows, local_lengths)
            return lax.map(per_micro, (query_dev, local_dev, carry_dev, length_dev))
        result = lax.map(per_device, (jnp.arange(N_RESP, dtype=jnp.int32), layer_queries, layer_local, carried, lengths))
        outputs.append(result.reshape(N_RESP * MB * TOKM, -1))
        carried = result
    return jnp.stack(outputs)
```

```python
import functools
import math

import jax
import jax.numpy as jnp
from jax import lax
from jax.experimental import pallas as pl
from jax.experimental.pallas import tpu as pltpu
from jax.sharding import PartitionSpec as P

HEAD = 128
GROUP_HEADS = 8
TOKM = 32
MB = 2
RESPS = 4
PROMPTS = 4
CHUNK = 8
EPS = 1e-06
MESH = pl.DeviceIdType.MESH
F32 = jnp.float32
BF16 = jnp.bfloat16


def kernel(
    sections,
    bits,
    q_hbm,
    r_hbm,
    p_hbm,
    owner,
    seg,
    out_hbm,
    q_v,
    r_v,
    p_v,
    vt_own,
    k_in,
    v_in,
    k_all,
    v_all,
    q_t,
    carry,
    sent,
    rows16,
    out_v,
    load_sem,
    out_sem,
    x_send,
    x_recv,
    c_send,
    c_recv,
):
    sec = lax.axis_index("section")
    place = lax.axis_index("resp")
    group = 1 << bits
    rank = lax.rem(place, group)
    block = lax.div(place, group)
    plen = p_v.shape[0]
    kvw = p_v.shape[1] // 2
    pairs = kvw // (2 * HEAD)
    near = r_v.shape[0]
    wide = pairs * 2 * GROUP_HEADS * HEAD
    chunks = near // CHUNK

    load_p = pltpu.make_async_copy(p_hbm.at[0], p_v, load_sem.at[0])
    load_q = pltpu.make_async_copy(q_hbm.at[0], q_v, load_sem.at[1])
    load_r = pltpu.make_async_copy(r_hbm.at[0], r_v, load_sem.at[2])
    load_p.start()
    load_q.start()
    load_r.start()

    partners = []
    for b in range(bits):
        bit = lax.rem(lax.div(place, 1 << b), 2)
        partners.append(place + (1 << b) * (1 - 2 * bit))

    barrier = pltpu.get_barrier_semaphore()
    for other in partners:
        pl.semaphore_signal(barrier, 1, device_id={"resp": other}, device_id_type=MESH)

    @pl.when(sec > 0)
    def _():
        pl.semaphore_signal(barrier, 1, device_id={"section": sec - 1}, device_id_type=MESH)

    @pl.when(sec < sections - 1)
    def _():
        pl.semaphore_signal(barrier, 1, device_id={"section": sec + 1}, device_id_type=MESH)

    @pl.when(sec == 0)
    def _():
        carry[...] = jnp.zeros_like(carry)

    load_p.wait()
    for g in range(kvw // HEAD):
        cols = slice(g * HEAD, (g + 1) * HEAD)
        vt_own[cols, :] = p_v[:, kvw + g * HEAD : kvw + (g + 1) * HEAD].T

    inside = (sec > 0) & (sec < sections - 1)

    @pl.when(inside)
    def _():
        pl.semaphore_wait(barrier, bits + 2)

    @pl.when(jnp.logical_not(inside))
    def _():
        pl.semaphore_wait(barrier, bits + 1)

    def exchange(b):
        if b == 0:
            sources = (p_v.at[:, 0:kvw], vt_own)
        else:
            sources = (k_all.at[0:plen, :], v_all.at[:, 0:plen])
        copies = []
        for n, (source, target) in enumerate(zip(sources, (k_in, v_in))):
            copies.append(
                pltpu.make_async_remote_copy(
                    src_ref=source,
                    dst_ref=target.at[b],
                    send_sem=x_send.at[b, n],
                    recv_sem=x_recv.at[b, n],
                    device_id={"resp": partners[b]},
                    device_id_type=MESH,
                )
            )
            copies[-1].start()
        return copies

    copies = exchange(0) if bits else None

    load_r.wait()
    load_q.wait()
    k_all[plen : plen + near, :] = r_v[:, 0:kvw]
    for g in range(kvw // HEAD):
        cols = slice(g * HEAD, (g + 1) * HEAD)
        v_all[cols, plen : plen + near] = r_v[:, kvw + g * HEAD : kvw + (g + 1) * HEAD].T

    def turn_queries(i, unused):
        both = q_v[pl.ds(pl.multiple_of(i * 16, 16), 16), :].astype(F32)
        for half in range(2):
            part = both[half * CHUNK : (half + 1) * CHUNK, :]
            for p in range(pairs):
                heads = [
                    part[:, (p * 16 + j) * HEAD : (p * 16 + j + 1) * HEAD] for j in range(16)
                ]
                q_t[2 * i + half, p * HEAD : (p + 1) * HEAD, :] = jnp.concatenate(heads, 0).T
        return unused

    lax.fori_loop(0, chunks // 2, turn_queries, 0)

    root = lax.rem(owner[0, block], group)
    if not bits:
        k_all[0:plen, :] = p_v[:, 0:kvw]
        v_all[:, 0:plen] = vt_own[...]
    for b in range(bits):
        if b:
            copies = exchange(b)
        keep = lax.div(rank, 1 << b) == lax.div(root, 1 << b)
        copies[0].wait()
        held = p_v[:, 0:kvw] if b == 0 else k_all[0:plen, :]
        k_all[0:plen, :] = jnp.where(keep, held, k_in[b])
        copies[1].wait()
        held = vt_own[...] if b == 0 else v_all[:, 0:plen]
        v_all[:, 0:plen] = jnp.where(keep, held, v_in[b])

    lane = lax.broadcasted_iota(jnp.int32, (1, HEAD), 1)
    lower = lane < HEAD // 2
    key_row = lax.broadcasted_iota(jnp.int32, (near, HEAD), 0)
    key_pos = lax.rem(key_row, TOKM)
    lane_row = lax.rem(lax.broadcasted_iota(jnp.int32, (near, HEAD), 1), CHUNK)
    factor = math.log2(math.e) / math.sqrt(HEAD)

    def forward(c):
        return pltpu.make_async_remote_copy(
            src_ref=sent.at[c],
            dst_ref=carry.at[c],
            send_sem=c_send.at[c],
            recv_sem=c_recv.at[c],
            device_id={"section": sec + 1},
            device_id_type=MESH,
        )

    def arrival(c):
        return pltpu.make_async_remote_copy(
            src_ref=sent.at[c],
            dst_ref=carry.at[c],
            send_sem=c_send.at[c],
            recv_sem=c_recv.at[c],
            device_id={"section": sec - 1},
            device_id_type=MESH,
        )

    def one_chunk(c, half):
        micro = lax.div(c * CHUNK, TOKM)
        row_pos = lane_row + lax.rem(c * CHUNK, TOKM)
        end = 0
        row_resp = jnp.zeros((near, HEAD), jnp.int32)
        key_resp = jnp.zeros((near, HEAD), jnp.int32)
        for n in range(RESPS):
            end = end + seg[micro, n]
            row_resp = row_resp + (row_pos >= end).astype(jnp.int32)
            key_resp = key_resp + (key_pos >= end).astype(jnp.int32)
        same_micro = lax.div(key_row, TOKM) == micro
        allowed = same_micro & (row_resp == key_resp) & (key_pos <= row_pos)

        @pl.when(sec > 0)
        def _():
            arrival(c).wait_recv()

        attended = []
        square = jnp.zeros((1, HEAD), F32)
        for p in range(pairs):
            part = slice(p * HEAD, (p + 1) * HEAD)
            both = slice(2 * p * HEAD, 2 * (p + 1) * HEAD)
            x = q_t[c, part, :] + carry[c, part, :].astype(F32)
            x = jnp.concatenate([jnp.where(lower, x, 0.0), jnp.where(lower, 0.0, x)], 0)
            s = jnp.dot(k_all[:, both], x.astype(BF16), preferred_element_type=F32)
            far, close = s[0:plen], jnp.where(allowed, s[plen:], -jnp.inf)
            top = jnp.maximum(
                jnp.max(far, axis=0, keepdims=True), jnp.max(close, axis=0, keepdims=True)
            )
            e = jnp.exp2((jnp.concatenate([far, close], 0) - top) * factor)
            total = jnp.sum(e, axis=0, keepdims=True)
            o = jnp.dot(v_all[both, :], e.astype(BF16), preferred_element_type=F32)
            o = jnp.where(lower, o[0:HEAD], o[HEAD:]) * (1.0 / total)
            attended.append(o)
            square = square + jnp.sum(o * o, axis=0, keepdims=True)
        square = jnp.broadcast_to(square, (8, HEAD))
        for distance in (8, 16, 32, 64):
            square = square + pltpu.roll(square, distance, 1)
        norm = lax.rsqrt(square[0:1] * (1.0 / wide) + EPS)
        for p in range(pairs):
            attended[p] = attended[p] * norm
            sent[c, p * HEAD : (p + 1) * HEAD, :] = attended[p].astype(BF16)

        @pl.when(sec < sections - 1)
        def _():
            forward(c).start()

        for p in range(pairs):
            turned = attended[p].T
            for j in range(16):
                rows16[
                    half * CHUNK : (half + 1) * CHUNK, (p * 16 + j) * HEAD : (p * 16 + j + 1) * HEAD
                ] = turned[j * CHUNK : (j + 1) * CHUNK, :]

    def store(i):
        rows = pl.ds(pl.multiple_of(i * 16, 16), 16)
        return pltpu.make_async_copy(out_v.at[rows, :], out_hbm.at[0, rows, :], out_sem.at[i])

    def two_chunks(i, unused):
        for half in range(2):
            one_chunk(2 * i + half, half)
        out_v[pl.ds(pl.multiple_of(i * 16, 16), 16), :] = rows16[...].astype(BF16)
        store(i).start()
        return unused

    lax.fori_loop(0, chunks // 2, two_chunks, 0)

    def finish(i, unused):
        store(i).wait()

        @pl.when(sec < sections - 1)
        def _():
            forward(2 * i).wait_send()
            forward(2 * i + 1).wait_send()

        return unused

    lax.fori_loop(0, chunks // 2, finish, 0)


def local(sections, bits, queries, resp_kv, prefix_kv, owner, seg_len):
    _, near, wide = queries.shape
    _, plen, kv2 = prefix_kv.shape
    kvw = kv2 // 2
    chunks = near // CHUNK
    pair_rows = kvw // 2
    steps = max(bits, 1)
    return pl.pallas_call(
        functools.partial(kernel, sections, bits),
        out_shape=jax.ShapeDtypeStruct(queries.shape, BF16),
        in_specs=[pl.BlockSpec(memory_space=pl.ANY)] * 3
        + [pl.BlockSpec(memory_space=pltpu.SMEM)] * 2,
        out_specs=pl.BlockSpec(memory_space=pl.ANY),
        scratch_shapes=[
            pltpu.VMEM((near, wide), BF16),
            pltpu.VMEM((near, kv2), BF16),
            pltpu.VMEM((plen, kv2), BF16),
            pltpu.VMEM((kvw, plen), BF16),
            pltpu.VMEM((steps, plen, kvw), BF16),
            pltpu.VMEM((steps, kvw, plen), BF16),
            pltpu.VMEM((plen + near, kvw), BF16),
            pltpu.VMEM((kvw, plen + near), BF16),
            pltpu.VMEM((chunks, pair_rows, HEAD), F32),
            pltpu.VMEM((chunks, pair_rows, HEAD), BF16),
            pltpu.VMEM((chunks, pair_rows, HEAD), BF16),
            pltpu.VMEM((16, wide), F32),
            pltpu.VMEM((near, wide), BF16),
            pltpu.SemaphoreType.DMA((3,)),
            pltpu.SemaphoreType.DMA((chunks // 2,)),
            pltpu.SemaphoreType.DMA((steps, 2)),
            pltpu.SemaphoreType.DMA((steps, 2)),
            pltpu.SemaphoreType.DMA((chunks,)),
            pltpu.SemaphoreType.DMA((chunks,)),
        ],
        compiler_params=pltpu.CompilerParams(
            collective_id=0, has_side_effects=True, vmem_limit_bytes=60 * 1024 * 1024
        ),
        cost_estimate=pl.CostEstimate(
            flops=4 * near * wide * (plen + TOKM),
            bytes_accessed=4 * near * wide + 2 * (plen + near) * kv2,
            transcendentals=near * (wide // HEAD) * (plen + TOKM),
        ),
        name="layers",
    )(queries, resp_kv, prefix_kv, owner, seg_len)


def solution(mesh):
    sections = mesh.shape["section"]
    group = mesh.shape["resp"] // PROMPTS
    return jax.shard_map(
        functools.partial(local, sections, group.bit_length() - 1),
        mesh=mesh,
        in_specs=(
            P("section", "resp", None),
            P("section", "resp", None),
            P("section", "resp", None),
            P("section", None),
            P("resp", None),
        ),
        out_specs=P("section", "resp", None),
        check_vma=False,
    )
```

```python
import functools
import math

import jax
import jax.numpy as jnp
from jax import lax
from jax.experimental import pallas as pl
from jax.experimental.pallas import tpu as pltpu
from jax.sharding import PartitionSpec as P

HEAD = 128
GROUP_HEADS = 8
TOKM = 32
MB = 2
RESPS = 4
PROMPTS = 4
CHUNK = 8
EPS = 1e-06
MESH = pl.DeviceIdType.MESH
F32 = jnp.float32
BF16 = jnp.bfloat16


def kernel(
    sections,
    bits,
    q_hbm,
    r_hbm,
    p_hbm,
    owner,
    seg,
    sent,
    q_v,
    r_v,
    p_v,
    vt_own,
    k_in,
    v_in,
    k_all,
    v_all,
    q_t,
    carry,
    bias,
    load_sem,
    x_send,
    x_recv,
    c_send,
    c_recv,
):
    sec = lax.axis_index("section")
    place = lax.axis_index("resp")
    group = 1 << bits
    rank = lax.rem(place, group)
    block = lax.div(place, group)
    plen = p_v.shape[0]
    kvw = p_v.shape[1] // 2
    pairs = kvw // (2 * HEAD)
    near = r_v.shape[0]
    wide = pairs * 2 * GROUP_HEADS * HEAD
    chunks = near // CHUNK

    load_p = pltpu.make_async_copy(p_hbm.at[0], p_v, load_sem.at[0])
    load_q = pltpu.make_async_copy(q_hbm.at[0], q_v, load_sem.at[1])
    load_r = pltpu.make_async_copy(r_hbm.at[0], r_v, load_sem.at[2])
    load_p.start()
    load_q.start()
    load_r.start()

    partners = []
    for b in range(bits):
        bit = lax.rem(lax.div(place, 1 << b), 2)
        partners.append(place + (1 << b) * (1 - 2 * bit))

    barrier = pltpu.get_barrier_semaphore()
    for other in partners:
        pl.semaphore_signal(barrier, 1, device_id={"resp": other}, device_id_type=MESH)

    @pl.when(sec > 0)
    def _():
        pl.semaphore_signal(barrier, 1, device_id={"section": sec - 1}, device_id_type=MESH)

    @pl.when(sec < sections - 1)
    def _():
        pl.semaphore_signal(barrier, 1, device_id={"section": sec + 1}, device_id_type=MESH)

    @pl.when(sec == 0)
    def _():
        carry[...] = jnp.zeros_like(carry)

    load_p.wait()
    for g in range(kvw // HEAD):
        cols = slice(g * HEAD, (g + 1) * HEAD)
        vt_own[cols, :] = p_v[:, kvw + g * HEAD : kvw + (g + 1) * HEAD].T

    inside = (sec > 0) & (sec < sections - 1)

    @pl.when(inside)
    def _():
        pl.semaphore_wait(barrier, bits + 2)

    @pl.when(jnp.logical_not(inside))
    def _():
        pl.semaphore_wait(barrier, bits + 1)

    def exchange(b):
        if b == 0:
            sources = (p_v.at[:, 0:kvw], vt_own)
        else:
            sources = (k_all.at[0:plen, :], v_all.at[:, 0:plen])
        copies = []
        for n, (source, target) in enumerate(zip(sources, (k_in, v_in))):
            copies.append(
                pltpu.make_async_remote_copy(
                    src_ref=source,
                    dst_ref=target.at[b],
                    send_sem=x_send.at[b, n],
                    recv_sem=x_recv.at[b, n],
                    device_id={"resp": partners[b]},
                    device_id_type=MESH,
                )
            )
            copies[-1].start()
        return copies

    copies = exchange(0) if bits else None

    load_r.wait()
    load_q.wait()
    k_all[plen : plen + near, :] = r_v[:, 0:kvw]
    for g in range(kvw // HEAD):
        cols = slice(g * HEAD, (g + 1) * HEAD)
        v_all[cols, plen : plen + near] = r_v[:, kvw + g * HEAD : kvw + (g + 1) * HEAD].T

    def turn_queries(i, unused):
        both = q_v[pl.ds(pl.multiple_of(i * 16, 16), 16), :].astype(F32)
        for half in range(2):
            part = both[half * CHUNK : (half + 1) * CHUNK, :]
            for p in range(pairs):
                heads = [
                    part[:, (p * 16 + j) * HEAD : (p * 16 + j + 1) * HEAD] for j in range(16)
                ]
                q_t[2 * i + half, p * HEAD : (p + 1) * HEAD, :] = jnp.concatenate(heads, 0).T
        return unused

    lax.fori_loop(0, chunks // 2, turn_queries, 0)

    lane = lax.broadcasted_iota(jnp.int32, (1, HEAD), 1)
    lower = lane < HEAD // 2
    lane_row = lane & (CHUNK - 1)
    key_row = lax.broadcasted_iota(jnp.int32, (near, HEAD), 0)
    key_pos = key_row & (TOKM - 1)
    for micro in range(MB):
        key_resp = jnp.where(key_row - key_pos == micro * TOKM, 0, -1)
        ends = []
        for n in range(RESPS):
            ends.append((ends[-1] if n else 0) + seg[micro, n])
            key_resp = key_resp + jnp.where((key_pos >= ends[n]) & (key_resp >= 0), 1, 0)
        for part in range(TOKM // CHUNK):
            row_pos = lane_row + part * CHUNK
            row_resp = jnp.zeros((1, HEAD), jnp.int32)
            for end in ends:
                row_resp = row_resp + jnp.where(row_pos >= end, 1, 0)
            allowed = (key_resp == row_resp) & (key_pos <= row_pos)
            bias[micro * (TOKM // CHUNK) + part] = jnp.where(allowed, 0.0, -jnp.inf)

    root = lax.rem(owner[0, block], group)
    if not bits:
        k_all[0:plen, :] = p_v[:, 0:kvw]
        v_all[:, 0:plen] = vt_own[...]
    for b in range(bits):
        if b:
            copies = exchange(b)
        keep = lax.div(rank, 1 << b) == lax.div(root, 1 << b)
        copies[0].wait()
        held = p_v[:, 0:kvw] if b == 0 else k_all[0:plen, :]
        k_all[0:plen, :] = jnp.where(keep, held, k_in[b])
        copies[1].wait()
        held = vt_own[...] if b == 0 else v_all[:, 0:plen]
        v_all[:, 0:plen] = jnp.where(keep, held, v_in[b])

    factor = math.log2(math.e) / math.sqrt(HEAD)

    def forward(c):
        return pltpu.make_async_remote_copy(
            src_ref=sent.at[c],
            dst_ref=carry.at[c],
            send_sem=c_send.at[c],
            recv_sem=c_recv.at[c],
            device_id={"section": sec + 1},
            device_id_type=MESH,
        )

    def arrival(c):
        return pltpu.make_async_remote_copy(
            src_ref=sent.at[c],
            dst_ref=carry.at[c],
            send_sem=c_send.at[c],
            recv_sem=c_recv.at[c],
            device_id={"section": sec - 1},
            device_id_type=MESH,
        )

    def one_chunk(c):
        @pl.when(sec > 0)
        def _():
            arrival(c).wait_recv()

        attended = []
        square = jnp.zeros((1, HEAD), F32)
        for p in range(pairs):
            part = slice(p * HEAD, (p + 1) * HEAD)
            both = slice(2 * p * HEAD, 2 * (p + 1) * HEAD)
            x = q_t[c, part, :] + carry[c, part, :].astype(F32)
            x = jnp.concatenate([jnp.where(lower, x, 0.0), jnp.where(lower, 0.0, x)], 0)
            s = jnp.dot(k_all[:, both], x.astype(BF16), preferred_element_type=F32)
            far, close = s[0:plen], s[plen:] + bias[c]
            top = jnp.maximum(
                jnp.max(far, axis=0, keepdims=True), jnp.max(close, axis=0, keepdims=True)
            )
            e = jnp.exp2((jnp.concatenate([far, close], 0) - top) * factor)
            total = jnp.sum(e, axis=0, keepdims=True)
            o = jnp.dot(v_all[both, :], e.astype(BF16), preferred_element_type=F32)
            o = jnp.where(lower, o[0:HEAD], o[HEAD:]) * (1.0 / total)
            attended.append(o)
            square = square + jnp.sum(o * o, axis=0, keepdims=True)
        square = jnp.broadcast_to(square, (8, HEAD))
        for distance in (8, 16, 32, 64):
            square = square + pltpu.roll(square, distance, 1)
        norm = lax.rsqrt(square[0:1] * (1.0 / wide) + EPS)
        for p in range(pairs):
            sent[c, p * HEAD : (p + 1) * HEAD, :] = (attended[p] * norm).astype(BF16)

        @pl.when(sec < sections - 1)
        def _():
            forward(c).start()

    def step(c, unused):
        one_chunk(c)
        return unused

    lax.fori_loop(0, chunks, step, 0)

    @pl.when(sec < sections - 1)
    def _():
        def finish(c, unused):
            forward(c).wait_send()
            return unused

        lax.fori_loop(0, chunks, finish, 0)


def turn_kernel(pairs, turned, out):
    for i in range(turned.shape[0] // 2):
        for p in range(pairs):
            part = slice(p * HEAD, (p + 1) * HEAD)
            first = turned[2 * i, part, :].astype(F32).T
            second = turned[2 * i + 1, part, :].astype(F32).T
            for j in range(16):
                rows = slice(j * CHUNK, (j + 1) * CHUNK)
                both = jnp.concatenate([first[rows], second[rows]], 0)
                column = (p * 16 + j) * HEAD
                out[0, 16 * i : 16 * (i + 1), column : column + HEAD] = both.astype(BF16)


def local(sections, bits, queries, resp_kv, prefix_kv, owner, seg_len):
    _, near, wide = queries.shape
    _, plen, kv2 = prefix_kv.shape
    kvw = kv2 // 2
    chunks = near // CHUNK
    pair_rows = kvw // 2
    steps = max(bits, 1)
    turned = pl.pallas_call(
        functools.partial(kernel, sections, bits),
        out_shape=jax.ShapeDtypeStruct((chunks, pair_rows, HEAD), BF16),
        in_specs=[pl.BlockSpec(memory_space=pl.ANY)] * 3
        + [pl.BlockSpec(memory_space=pltpu.SMEM)] * 2,
        out_specs=pl.BlockSpec(memory_space=pltpu.VMEM),
        scratch_shapes=[
            pltpu.VMEM((near, wide), BF16),
            pltpu.VMEM((near, kv2), BF16),
            pltpu.VMEM((plen, kv2), BF16),
            pltpu.VMEM((kvw, plen), BF16),
            pltpu.VMEM((steps, plen, kvw), BF16),
            pltpu.VMEM((steps, kvw, plen), BF16),
            pltpu.VMEM((plen + near, kvw), BF16),
            pltpu.VMEM((kvw, plen + near), BF16),
            pltpu.VMEM((chunks, pair_rows, HEAD), F32),
            pltpu.VMEM((chunks, pair_rows, HEAD), BF16),
            pltpu.VMEM((chunks, near, HEAD), F32),
            pltpu.SemaphoreType.DMA((3,)),
            pltpu.SemaphoreType.DMA((steps, 2)),
            pltpu.SemaphoreType.DMA((steps, 2)),
            pltpu.SemaphoreType.DMA((chunks,)),
            pltpu.SemaphoreType.DMA((chunks,)),
        ],
        compiler_params=pltpu.CompilerParams(
            collective_id=0, has_side_effects=True, vmem_limit_bytes=60 * 1024 * 1024
        ),
        cost_estimate=pl.CostEstimate(
            flops=4 * near * wide * (plen + TOKM),
            bytes_accessed=4 * near * wide + 2 * (plen + near) * kv2,
            transcendentals=near * (wide // HEAD) * (plen + TOKM),
        ),
        name="layers",
    )(queries, resp_kv, prefix_kv, owner, seg_len)
    parts = 2
    return pl.pallas_call(
        functools.partial(turn_kernel, kvw // (2 * HEAD)),
        grid=(parts,),
        out_shape=jax.ShapeDtypeStruct(queries.shape, BF16),
        in_specs=[pl.BlockSpec((chunks // parts, pair_rows, HEAD), lambda i: (i, 0, 0))],
        out_specs=pl.BlockSpec((1, near // parts, wide), lambda i: (0, i, 0)),
        name="turn",
    )(turned)


def solution(mesh):
    sections = mesh.shape["section"]
    group = mesh.shape["resp"] // PROMPTS
    return jax.shard_map(
        functools.partial(local, sections, group.bit_length() - 1),
        mesh=mesh,
        in_specs=(
            P("section", "resp", None),
            P("section", "resp", None),
            P("section", "resp", None),
            P("section", None),
            P("resp", None),
        ),
        out_specs=P("section", "resp", None),
        check_vma=False,
    )
```

```python
import functools
import math

import jax
import jax.numpy as jnp
from jax import lax
from jax.experimental import pallas as pl
from jax.experimental.pallas import tpu as pltpu
from jax.sharding import PartitionSpec as P

HEAD = 128
GROUP_HEADS = 8
TOKM = 32
MB = 2
RESPS = 4
PROMPTS = 4
CHUNK = 8
EPS = 1e-06
MESH = pl.DeviceIdType.MESH
F32 = jnp.float32
BF16 = jnp.bfloat16


def kernel(
    sections,
    bits,
    q_hbm,
    r_hbm,
    p_hbm,
    owner,
    seg,
    done_hbm,
    q_v,
    r_v,
    p_v,
    vt_own,
    k_in,
    v_in,
    k_all,
    v_all,
    q_t,
    carry,
    sent,
    bias,
    load_sem,
    done_sem,
    x_send,
    x_recv,
    c_send,
    c_recv,
):
    sec = lax.axis_index("section")
    place = lax.axis_index("resp")
    group = 1 << bits
    rank = lax.rem(place, group)
    block = lax.div(place, group)
    plen = p_v.shape[0]
    kvw = p_v.shape[1] // 2
    pairs = kvw // (2 * HEAD)
    near = r_v.shape[0]
    wide = pairs * 2 * GROUP_HEADS * HEAD
    chunks = near // CHUNK

    load_p = pltpu.make_async_copy(p_hbm.at[0], p_v, load_sem.at[0])
    load_q = pltpu.make_async_copy(q_hbm.at[0], q_v, load_sem.at[1])
    load_r = pltpu.make_async_copy(r_hbm.at[0], r_v, load_sem.at[2])
    load_p.start()
    load_q.start()
    load_r.start()

    partners = []
    for b in range(bits):
        bit = lax.rem(lax.div(place, 1 << b), 2)
        partners.append(place + (1 << b) * (1 - 2 * bit))

    barrier = pltpu.get_barrier_semaphore()
    for other in partners:
        pl.semaphore_signal(barrier, 1, device_id={"resp": other}, device_id_type=MESH)

    @pl.when(sec > 0)
    def _():
        pl.semaphore_signal(barrier, 1, device_id={"section": sec - 1}, device_id_type=MESH)

    @pl.when(sec < sections - 1)
    def _():
        pl.semaphore_signal(barrier, 1, device_id={"section": sec + 1}, device_id_type=MESH)

    @pl.when(sec == 0)
    def _():
        carry[...] = jnp.zeros_like(carry)

    def turn_values(p):
        for g in (2 * p, 2 * p + 1):
            cols = slice(g * HEAD, (g + 1) * HEAD)
            vt_own[cols, :] = p_v[:, kvw + g * HEAD : kvw + (g + 1) * HEAD].T

    load_p.wait()
    turn_values(0)

    inside = (sec > 0) & (sec < sections - 1)

    @pl.when(inside)
    def _():
        pl.semaphore_wait(barrier, bits + 2)

    @pl.when(jnp.logical_not(inside))
    def _():
        pl.semaphore_wait(barrier, bits + 1)

    def exchange(b, p):
        both = slice(2 * p * HEAD, 2 * (p + 1) * HEAD)
        if b == 0:
            sources = (p_v.at[:, both], vt_own.at[both, :])
        else:
            sources = (k_all.at[0:plen, both], v_all.at[both, 0:plen])
        targets = (k_in.at[b, :, both], v_in.at[b, both, :])
        copies = []
        for n, (source, target) in enumerate(zip(sources, targets)):
            copies.append(
                pltpu.make_async_remote_copy(
                    src_ref=source,
                    dst_ref=target,
                    send_sem=x_send.at[b, p, n],
                    recv_sem=x_recv.at[b, p, n],
                    device_id={"resp": partners[b]},
                    device_id_type=MESH,
                )
            )
            copies[-1].start()
        return copies

    first = []
    for p in range(pairs):
        if p:
            turn_values(p)
        if bits:
            first.append(exchange(0, p))

    load_r.wait()
    load_q.wait()
    k_all[plen : plen + near, :] = r_v[:, 0:kvw]
    for g in range(kvw // HEAD):
        cols = slice(g * HEAD, (g + 1) * HEAD)
        v_all[cols, plen : plen + near] = r_v[:, kvw + g * HEAD : kvw + (g + 1) * HEAD].T

    def turn_queries(i, unused):
        both = q_v[pl.ds(pl.multiple_of(i * 16, 16), 16), :].astype(F32)
        for half in range(2):
            part = both[half * CHUNK : (half + 1) * CHUNK, :]
            for p in range(pairs):
                heads = [
                    part[:, (p * 16 + j) * HEAD : (p * 16 + j + 1) * HEAD] for j in range(16)
                ]
                q_t[2 * i + half, p * HEAD : (p + 1) * HEAD, :] = jnp.concatenate(heads, 0).T
        return unused

    lax.fori_loop(0, chunks // 2, turn_queries, 0)

    lane = lax.broadcasted_iota(jnp.int32, (1, HEAD), 1)
    lower = lane < HEAD // 2
    lane_row = lane & (CHUNK - 1)
    key_row = lax.broadcasted_iota(jnp.int32, (near, HEAD), 0)
    key_pos = key_row & (TOKM - 1)
    for micro in range(MB):
        key_resp = jnp.where(key_row - key_pos == micro * TOKM, 0, -1)
        ends = []
        for n in range(RESPS):
            ends.append((ends[-1] if n else 0) + seg[micro, n])
            key_resp = key_resp + jnp.where((key_pos >= ends[n]) & (key_resp >= 0), 1, 0)
        for part in range(TOKM // CHUNK):
            row_pos = lane_row + part * CHUNK
            row_resp = jnp.zeros((1, HEAD), jnp.int32)
            for end in ends:
                row_resp = row_resp + jnp.where(row_pos >= end, 1, 0)
            allowed = (key_resp == row_resp) & (key_pos <= row_pos)
            bias[micro * (TOKM // CHUNK) + part] = jnp.where(allowed, 0.0, -jnp.inf)

    root = lax.rem(owner[0, block], group)

    def settle(b, p, copies):
        both = slice(2 * p * HEAD, 2 * (p + 1) * HEAD)
        keep = lax.div(rank, 1 << b) == lax.div(root, 1 << b)
        copies[0].wait()
        held = p_v[:, both] if b == 0 else k_all[0:plen, both]
        k_all[0:plen, both] = jnp.where(keep, held, k_in[b, :, both])
        copies[1].wait()
        held = vt_own[both, :] if b == 0 else v_all[both, 0:plen]
        v_all[both, 0:plen] = jnp.where(keep, held, v_in[b, both, :])

    def prefix_ready(p):
        both = slice(2 * p * HEAD, 2 * (p + 1) * HEAD)
        if not bits:
            k_all[0:plen, both] = p_v[:, both]
            v_all[both, 0:plen] = vt_own[both, :]
        for b in range(bits):
            settle(b, p, first[p] if b == 0 else exchange(b, p))

    factor = math.log2(math.e) / math.sqrt(HEAD)

    def forward(c):
        return pltpu.make_async_remote_copy(
            src_ref=sent.at[c],
            dst_ref=carry.at[c],
            send_sem=c_send.at[c],
            recv_sem=c_recv.at[c],
            device_id={"section": sec + 1},
            device_id_type=MESH,
        )

    def arrival(c):
        return pltpu.make_async_remote_copy(
            src_ref=sent.at[c],
            dst_ref=carry.at[c],
            send_sem=c_send.at[c],
            recv_sem=c_recv.at[c],
            device_id={"section": sec - 1},
            device_id_type=MESH,
        )

    def done(c):
        return pltpu.make_async_copy(sent.at[c], done_hbm.at[c], done_sem.at[c])

    def one_chunk(c, ready=None):
        @pl.when(sec > 0)
        def _():
            arrival(c).wait_recv()

        attended = []
        square = jnp.zeros((1, HEAD), F32)
        for p in range(pairs):
            part = slice(p * HEAD, (p + 1) * HEAD)
            both = slice(2 * p * HEAD, 2 * (p + 1) * HEAD)
            if ready is not None:
                ready(p)
            x = q_t[c, part, :] + carry[c, part, :].astype(F32)
            x = jnp.concatenate([jnp.where(lower, x, 0.0), jnp.where(lower, 0.0, x)], 0)
            s = jnp.dot(k_all[:, both], x.astype(BF16), preferred_element_type=F32)
            far, close = s[0:plen], s[plen:] + bias[c]
            top = jnp.maximum(
                jnp.max(far, axis=0, keepdims=True), jnp.max(close, axis=0, keepdims=True)
            )
            e = jnp.exp2((jnp.concatenate([far, close], 0) - top) * factor)
            total = jnp.sum(e, axis=0, keepdims=True)
            e = e * (1.0 / total)
            o = jnp.dot(v_all[both, :], e.astype(BF16), preferred_element_type=F32)
            o = jnp.where(lower, o[0:HEAD], o[HEAD:])
            attended.append(o)
            square = square + jnp.sum(o * o, axis=0, keepdims=True)
        square = jnp.broadcast_to(square, (8, HEAD))
        for distance in (8, 16, 32, 64):
            square = square + pltpu.roll(square, distance, 1)
        norm = lax.rsqrt(square[0:1] * (1.0 / wide) + EPS)
        for p in range(pairs):
            sent[c, p * HEAD : (p + 1) * HEAD, :] = (attended[p] * norm).astype(BF16)

        @pl.when(sec < sections - 1)
        def _():
            forward(c).start()

        done(c).start()

    def step(c, unused):
        one_chunk(c)
        return unused

    one_chunk(0, prefix_ready)
    lax.fori_loop(1, chunks, step, 0)

    def finish(c, unused):
        done(c).wait()

        @pl.when(sec < sections - 1)
        def _():
            forward(c).wait_send()

        return unused

    lax.fori_loop(0, chunks, finish, 0)


def turn_kernel(pairs, turned_hbm, out_hbm, turned, out, in_sem, out_sem):
    parts = turned.shape[0] // 2
    loads, stores = [], []
    for i in range(parts):
        chunk = slice(2 * i, 2 * i + 2)
        loads.append(pltpu.make_async_copy(turned_hbm.at[chunk], turned.at[chunk], in_sem.at[i]))
        loads[-1].start()
    for i in range(parts):
        loads[i].wait()
        for p in range(pairs):
            part = slice(p * HEAD, (p + 1) * HEAD)
            first = turned[2 * i, part, :].astype(F32).T
            second = turned[2 * i + 1, part, :].astype(F32).T
            for j in range(16):
                rows = slice(j * CHUNK, (j + 1) * CHUNK)
                both = jnp.concatenate([first[rows], second[rows]], 0)
                column = (p * 16 + j) * HEAD
                out[16 * i : 16 * (i + 1), column : column + HEAD] = both.astype(BF16)
        rows = slice(16 * i, 16 * (i + 1))
        stores.append(pltpu.make_async_copy(out.at[rows], out_hbm.at[0, rows], out_sem.at[i]))
        stores[-1].start()
    for copy in stores:
        copy.wait()


def local(sections, bits, queries, resp_kv, prefix_kv, owner, seg_len):
    _, near, wide = queries.shape
    _, plen, kv2 = prefix_kv.shape
    kvw = kv2 // 2
    chunks = near // CHUNK
    pair_rows = kvw // 2
    steps = max(bits, 1)
    turned = pl.pallas_call(
        functools.partial(kernel, sections, bits),
        out_shape=jax.ShapeDtypeStruct((chunks, pair_rows, HEAD), BF16),
        in_specs=[pl.BlockSpec(memory_space=pl.ANY)] * 3
        + [pl.BlockSpec(memory_space=pltpu.SMEM)] * 2,
        out_specs=pl.BlockSpec(memory_space=pl.ANY),
        scratch_shapes=[
            pltpu.VMEM((near, wide), BF16),
            pltpu.VMEM((near, kv2), BF16),
            pltpu.VMEM((plen, kv2), BF16),
            pltpu.VMEM((kvw, plen), BF16),
            pltpu.VMEM((steps, plen, kvw), BF16),
            pltpu.VMEM((steps, kvw, plen), BF16),
            pltpu.VMEM((plen + near, kvw), BF16),
            pltpu.VMEM((kvw, plen + near), BF16),
            pltpu.VMEM((chunks, pair_rows, HEAD), F32),
            pltpu.VMEM((chunks, pair_rows, HEAD), BF16),
            pltpu.VMEM((chunks, pair_rows, HEAD), BF16),
            pltpu.VMEM((chunks, near, HEAD), F32),
            pltpu.SemaphoreType.DMA((3,)),
            pltpu.SemaphoreType.DMA((chunks,)),
            pltpu.SemaphoreType.DMA((steps, 2, 2)),
            pltpu.SemaphoreType.DMA((steps, 2, 2)),
            pltpu.SemaphoreType.DMA((chunks,)),
            pltpu.SemaphoreType.DMA((chunks,)),
        ],
        compiler_params=pltpu.CompilerParams(
            collective_id=0, has_side_effects=True, vmem_limit_bytes=60 * 1024 * 1024
        ),
        cost_estimate=pl.CostEstimate(
            flops=4 * near * wide * (plen + TOKM),
            bytes_accessed=4 * near * wide + 2 * (plen + near) * kv2,
            transcendentals=near * (wide // HEAD) * (plen + TOKM),
        ),
        name="layers",
    )(queries, resp_kv, prefix_kv, owner, seg_len)
    return pl.pallas_call(
        functools.partial(turn_kernel, kvw // (2 * HEAD)),
        out_shape=jax.ShapeDtypeStruct(queries.shape, BF16),
        in_specs=[pl.BlockSpec(memory_space=pl.ANY)],
        out_specs=pl.BlockSpec(memory_space=pl.ANY),
        scratch_shapes=[
            pltpu.VMEM((chunks, pair_rows, HEAD), BF16),
            pltpu.VMEM((near, wide), BF16),
            pltpu.SemaphoreType.DMA((chunks // 2,)),
            pltpu.SemaphoreType.DMA((chunks // 2,)),
        ],
        compiler_params=pltpu.CompilerParams(vmem_limit_bytes=60 * 1024 * 1024),
        name="turn",
    )(turned)


def solution(mesh):
    sections = mesh.shape["section"]
    group = mesh.shape["resp"] // PROMPTS
    return jax.shard_map(
        functools.partial(local, sections, group.bit_length() - 1),
        mesh=mesh,
        in_specs=(
            P("section", "resp", None),
            P("section", "resp", None),
            P("section", "resp", None),
            P("section", None),
            P("resp", None),
        ),
        out_specs=P("section", "resp", None),
        check_vma=False,
    )
```

```python
import functools
import math

import jax
import jax.numpy as jnp
from jax import lax
from jax.experimental import pallas as pl
from jax.experimental.pallas import tpu as pltpu
from jax.sharding import PartitionSpec as P

HEAD = 128
GROUP_HEADS = 8
TOKM = 32
MB = 2
RESPS = 4
PROMPTS = 4
CHUNK = 8
EPS = 1e-06
MESH = pl.DeviceIdType.MESH
F32 = jnp.float32
BF16 = jnp.bfloat16


def kernel(
    sections,
    bits,
    q_hbm,
    r_hbm,
    p_hbm,
    owner,
    seg,
    done_hbm,
    q_v,
    r_v,
    p_v,
    vt_own,
    k_in,
    v_in,
    k_all,
    v_all,
    q_t,
    carry,
    sent,
    bias,
    load_sem,
    done_sem,
    x_send,
    x_recv,
    c_send,
    c_recv,
):
    sec = lax.axis_index("section")
    place = lax.axis_index("resp")
    group = 1 << bits
    rank = lax.rem(place, group)
    block = lax.div(place, group)
    plen = p_v.shape[0]
    kvw = p_v.shape[1] // 2
    pairs = kvw // (2 * HEAD)
    near = r_v.shape[0]
    wide = pairs * 2 * GROUP_HEADS * HEAD
    chunks = near // CHUNK

    load_p = pltpu.make_async_copy(p_hbm.at[0], p_v, load_sem.at[0])
    load_q = pltpu.make_async_copy(q_hbm.at[0], q_v, load_sem.at[1])
    load_r = pltpu.make_async_copy(r_hbm.at[0], r_v, load_sem.at[2])
    load_p.start()
    load_q.start()
    load_r.start()

    partners = []
    for b in range(bits):
        bit = lax.rem(lax.div(place, 1 << b), 2)
        partners.append(place + (1 << b) * (1 - 2 * bit))

    barrier = pltpu.get_barrier_semaphore()
    for other in partners:
        pl.semaphore_signal(barrier, 1, device_id={"resp": other}, device_id_type=MESH)

    @pl.when(sec > 0)
    def _():
        pl.semaphore_signal(barrier, 1, device_id={"section": sec - 1}, device_id_type=MESH)

    @pl.when(sec < sections - 1)
    def _():
        pl.semaphore_signal(barrier, 1, device_id={"section": sec + 1}, device_id_type=MESH)

    @pl.when(sec == 0)
    def _():
        carry[...] = jnp.zeros_like(carry)

    def turn_values(p):
        for g in (2 * p, 2 * p + 1):
            cols = slice(g * HEAD, (g + 1) * HEAD)
            vt_own[cols, :] = p_v[:, kvw + g * HEAD : kvw + (g + 1) * HEAD].T

    load_p.wait()
    turn_values(0)

    inside = (sec > 0) & (sec < sections - 1)

    @pl.when(inside)
    def _():
        pl.semaphore_wait(barrier, bits + 2)

    @pl.when(jnp.logical_not(inside))
    def _():
        pl.semaphore_wait(barrier, bits + 1)

    def exchange(b, p):
        both = slice(2 * p * HEAD, 2 * (p + 1) * HEAD)
        if b == 0:
            sources = (p_v.at[:, both], vt_own.at[both, :])
        else:
            sources = (k_all.at[0:plen, both], v_all.at[both, 0:plen])
        targets = (k_in.at[b, :, both], v_in.at[b, both, :])
        copies = []
        for n, (source, target) in enumerate(zip(sources, targets)):
            copies.append(
                pltpu.make_async_remote_copy(
                    src_ref=source,
                    dst_ref=target,
                    send_sem=x_send.at[b, p, n],
                    recv_sem=x_recv.at[b, p, n],
                    device_id={"resp": partners[b]},
                    device_id_type=MESH,
                )
            )
            copies[-1].start()
        return copies

    first = []
    for p in range(pairs):
        if p:
            turn_values(p)
        if bits:
            first.append(exchange(0, p))

    load_r.wait()
    load_q.wait()
    k_all[plen : plen + near, :] = r_v[:, 0:kvw]
    for g in range(kvw // HEAD):
        cols = slice(g * HEAD, (g + 1) * HEAD)
        v_all[cols, plen : plen + near] = r_v[:, kvw + g * HEAD : kvw + (g + 1) * HEAD].T

    def turn_queries(i, unused):
        both = q_v[pl.ds(pl.multiple_of(i * 16, 16), 16), :].astype(F32)
        for half in range(2):
            part = both[half * CHUNK : (half + 1) * CHUNK, :]
            for p in range(pairs):
                heads = [
                    part[:, (p * 16 + j) * HEAD : (p * 16 + j + 1) * HEAD] for j in range(16)
                ]
                q_t[2 * i + half, p * HEAD : (p + 1) * HEAD, :] = jnp.concatenate(heads, 0).T
        return unused

    lax.fori_loop(0, chunks // 2, turn_queries, 0)

    lane = lax.broadcasted_iota(jnp.int32, (1, HEAD), 1)
    lower = lane < HEAD // 2
    lane_row = lane & (CHUNK - 1)
    key_row = lax.broadcasted_iota(jnp.int32, (near, HEAD), 0)
    key_pos = key_row & (TOKM - 1)
    for micro in range(MB):
        key_resp = jnp.where(key_row - key_pos == micro * TOKM, 0, -1)
        ends = []
        for n in range(RESPS):
            ends.append((ends[-1] if n else 0) + seg[micro, n])
            key_resp = key_resp + jnp.where((key_pos >= ends[n]) & (key_resp >= 0), 1, 0)
        for part in range(TOKM // CHUNK):
            row_pos = lane_row + part * CHUNK
            row_resp = jnp.zeros((1, HEAD), jnp.int32)
            for end in ends:
                row_resp = row_resp + jnp.where(row_pos >= end, 1, 0)
            allowed = (key_resp == row_resp) & (key_pos <= row_pos)
            bias[micro * (TOKM // CHUNK) + part] = jnp.where(allowed, 0.0, -jnp.inf)

    root = lax.rem(owner[0, block], group)

    def settle(b, p, copies):
        both = slice(2 * p * HEAD, 2 * (p + 1) * HEAD)
        keep = lax.div(rank, 1 << b) == lax.div(root, 1 << b)
        copies[0].wait()
        held = p_v[:, both] if b == 0 else k_all[0:plen, both]
        k_all[0:plen, both] = jnp.where(keep, held, k_in[b, :, both])
        copies[1].wait()
        held = vt_own[both, :] if b == 0 else v_all[both, 0:plen]
        v_all[both, 0:plen] = jnp.where(keep, held, v_in[b, both, :])

    def prefix_ready(p):
        both = slice(2 * p * HEAD, 2 * (p + 1) * HEAD)
        if not bits:
            k_all[0:plen, both] = p_v[:, both]
            v_all[both, 0:plen] = vt_own[both, :]
        for b in range(bits):
            settle(b, p, first[p] if b == 0 else exchange(b, p))

    factor = math.log2(math.e) / math.sqrt(HEAD)

    def forward(c):
        return pltpu.make_async_remote_copy(
            src_ref=sent.at[c],
            dst_ref=carry.at[c],
            send_sem=c_send.at[c],
            recv_sem=c_recv.at[c],
            device_id={"section": sec + 1},
            device_id_type=MESH,
        )

    def arrival(c):
        return pltpu.make_async_remote_copy(
            src_ref=sent.at[c],
            dst_ref=carry.at[c],
            send_sem=c_send.at[c],
            recv_sem=c_recv.at[c],
            device_id={"section": sec - 1},
            device_id_type=MESH,
        )

    def done(c):
        return pltpu.make_async_copy(sent.at[c], done_hbm.at[c], done_sem.at[c])

    def one_chunk(c, ready=None):
        @pl.when(sec > 0)
        def _():
            arrival(c).wait_recv()

        attended = []
        square = jnp.zeros((1, HEAD), F32)
        for p in range(pairs):
            part = slice(p * HEAD, (p + 1) * HEAD)
            both = slice(2 * p * HEAD, 2 * (p + 1) * HEAD)
            if ready is not None:
                ready(p)
            x = q_t[c, part, :] + carry[c, part, :].astype(F32)
            x = jnp.concatenate([jnp.where(lower, x, 0.0), jnp.where(lower, 0.0, x)], 0)
            s = jnp.dot(k_all[:, both], x.astype(BF16), preferred_element_type=F32)
            far, close = s[0:plen], s[plen:] + bias[c]
            top = jnp.maximum(
                jnp.max(far, axis=0, keepdims=True), jnp.max(close, axis=0, keepdims=True)
            )
            e = jnp.exp2((jnp.concatenate([far, close], 0) - top) * factor)
            total = jnp.sum(e, axis=0, keepdims=True)
            o = jnp.dot(v_all[both, :], e.astype(BF16), preferred_element_type=F32)
            o = jnp.where(lower, o[0:HEAD], o[HEAD:]) * (1.0 / total)
            attended.append(o)
            square = square + jnp.sum(o * o, axis=0, keepdims=True)
        square = jnp.broadcast_to(square, (8, HEAD))
        for distance in (8, 16, 32, 64):
            square = square + pltpu.roll(square, distance, 1)
        norm = lax.rsqrt(square[0:1] * (1.0 / wide) + EPS)
        for p in range(pairs):
            sent[c, p * HEAD : (p + 1) * HEAD, :] = (attended[p] * norm).astype(BF16)

        @pl.when(sec < sections - 1)
        def _():
            forward(c).start()

        done(c).start()

    def step(c, unused):
        one_chunk(c)
        return unused

    one_chunk(0, prefix_ready)
    lax.fori_loop(1, chunks, step, 0)

    def finish(c, unused):
        done(c).wait()

        @pl.when(sec < sections - 1)
        def _():
            forward(c).wait_send()

        return unused

    lax.fori_loop(0, chunks, finish, 0)


def turn_kernel(pairs, turned_hbm, out_hbm, turned, out, in_sem, out_sem):
    parts = turned.shape[0] // 2
    loads, stores = [], []
    for i in range(parts):
        chunk = slice(2 * i, 2 * i + 2)
        loads.append(pltpu.make_async_copy(turned_hbm.at[chunk], turned.at[chunk], in_sem.at[i]))
        loads[-1].start()
    for i in range(parts):
        loads[i].wait()
        for p in range(pairs):
            part = slice(p * HEAD, (p + 1) * HEAD)
            first = turned[2 * i, part, :].astype(F32).T
            second = turned[2 * i + 1, part, :].astype(F32).T
            for j in range(16):
                rows = slice(j * CHUNK, (j + 1) * CHUNK)
                both = jnp.concatenate([first[rows], second[rows]], 0)
                column = (p * 16 + j) * HEAD
                out[16 * i : 16 * (i + 1), column : column + HEAD] = both.astype(BF16)
        rows = slice(16 * i, 16 * (i + 1))
        stores.append(pltpu.make_async_copy(out.at[rows], out_hbm.at[0, rows], out_sem.at[i]))
        stores[-1].start()
    for copy in stores:
        copy.wait()


def local(sections, bits, queries, resp_kv, prefix_kv, owner, seg_len):
    _, near, wide = queries.shape
    _, plen, kv2 = prefix_kv.shape
    kvw = kv2 // 2
    chunks = near // CHUNK
    pair_rows = kvw // 2
    steps = max(bits, 1)
    turned = pl.pallas_call(
        functools.partial(kernel, sections, bits),
        out_shape=jax.ShapeDtypeStruct((chunks, pair_rows, HEAD), BF16),
        in_specs=[pl.BlockSpec(memory_space=pl.ANY)] * 3
        + [pl.BlockSpec(memory_space=pltpu.SMEM)] * 2,
        out_specs=pl.BlockSpec(memory_space=pl.ANY),
        scratch_shapes=[
            pltpu.VMEM((near, wide), BF16),
            pltpu.VMEM((near, kv2), BF16),
            pltpu.VMEM((plen, kv2), BF16),
            pltpu.VMEM((kvw, plen), BF16),
            pltpu.VMEM((steps, plen, kvw), BF16),
            pltpu.VMEM((steps, kvw, plen), BF16),
            pltpu.VMEM((plen + near, kvw), BF16),
            pltpu.VMEM((kvw, plen + near), BF16),
            pltpu.VMEM((chunks, pair_rows, HEAD), F32),
            pltpu.VMEM((chunks, pair_rows, HEAD), BF16),
            pltpu.VMEM((chunks, pair_rows, HEAD), BF16),
            pltpu.VMEM((chunks, near, HEAD), F32),
            pltpu.SemaphoreType.DMA((3,)),
            pltpu.SemaphoreType.DMA((chunks,)),
            pltpu.SemaphoreType.DMA((steps, 2, 2)),
            pltpu.SemaphoreType.DMA((steps, 2, 2)),
            pltpu.SemaphoreType.DMA((chunks,)),
            pltpu.SemaphoreType.DMA((chunks,)),
        ],
        compiler_params=pltpu.CompilerParams(
            collective_id=0, has_side_effects=True, vmem_limit_bytes=60 * 1024 * 1024
        ),
        cost_estimate=pl.CostEstimate(
            flops=4 * near * wide * (plen + TOKM),
            bytes_accessed=4 * near * wide + 2 * (plen + near) * kv2,
            transcendentals=near * (wide // HEAD) * (plen + TOKM),
        ),
        name="layers",
    )(queries, resp_kv, prefix_kv, owner, seg_len)
    return pl.pallas_call(
        functools.partial(turn_kernel, kvw // (2 * HEAD)),
        out_shape=jax.ShapeDtypeStruct(queries.shape, BF16),
        in_specs=[pl.BlockSpec(memory_space=pl.ANY)],
        out_specs=pl.BlockSpec(memory_space=pl.ANY),
        scratch_shapes=[
            pltpu.VMEM((chunks, pair_rows, HEAD), BF16),
            pltpu.VMEM((near, wide), BF16),
            pltpu.SemaphoreType.DMA((chunks // 2,)),
            pltpu.SemaphoreType.DMA((chunks // 2,)),
        ],
        compiler_params=pltpu.CompilerParams(vmem_limit_bytes=60 * 1024 * 1024),
        name="turn",
    )(turned)


def solution(mesh):
    sections = mesh.shape["section"]
    group = mesh.shape["resp"] // PROMPTS
    return jax.shard_map(
        functools.partial(local, sections, group.bit_length() - 1),
        mesh=mesh,
        in_specs=(
            P("section", "resp", None),
            P("section", "resp", None),
            P("section", "resp", None),
            P("section", None),
            P("resp", None),
        ),
        out_specs=P("section", "resp", None),
        check_vma=False,
    )
```

```python
import functools
import math

import jax
import jax.numpy as jnp
from jax import lax
from jax.experimental import pallas as pl
from jax.experimental.pallas import tpu as pltpu
from jax.sharding import PartitionSpec as P

HEAD = 128
GROUP_HEADS = 8
TOKM = 32
MB = 2
RESPS = 4
PROMPTS = 4
CHUNK = 8
EPS = 1e-06
MESH = pl.DeviceIdType.MESH
F32 = jnp.float32
BF16 = jnp.bfloat16


def kernel(
    sections,
    bits,
    q_hbm,
    r_hbm,
    p_hbm,
    owner,
    seg,
    sent,
    q_v,
    r_v,
    p_v,
    kv_in,
    kv_all,
    q_t,
    carry,
    bias,
    load_sem,
    x_send,
    x_recv,
    c_send,
    c_recv,
):
    sec = lax.axis_index("section")
    place = lax.axis_index("resp")
    group = 1 << bits
    rank = lax.rem(place, group)
    block = lax.div(place, group)
    plen = p_v.shape[0]
    kvw = p_v.shape[1] // 2
    pairs = kvw // (2 * HEAD)
    near = r_v.shape[0]
    wide = pairs * 2 * GROUP_HEADS * HEAD
    chunks = near // CHUNK

    load_p = pltpu.make_async_copy(p_hbm.at[0], p_v, load_sem.at[0])
    load_q = pltpu.make_async_copy(q_hbm.at[0], q_v, load_sem.at[1])
    load_r = pltpu.make_async_copy(r_hbm.at[0], r_v, load_sem.at[2])
    load_p.start()
    load_q.start()
    load_r.start()

    partners = []
    for b in range(bits):
        bit = lax.rem(lax.div(place, 1 << b), 2)
        partners.append(place + (1 << b) * (1 - 2 * bit))

    barrier = pltpu.get_barrier_semaphore()
    for other in partners:
        pl.semaphore_signal(barrier, 1, device_id={"resp": other}, device_id_type=MESH)

    @pl.when(sec > 0)
    def _():
        pl.semaphore_signal(barrier, 1, device_id={"section": sec - 1}, device_id_type=MESH)

    @pl.when(sec < sections - 1)
    def _():
        pl.semaphore_signal(barrier, 1, device_id={"section": sec + 1}, device_id_type=MESH)

    @pl.when(sec == 0)
    def _():
        carry[...] = jnp.zeros_like(carry)

    load_p.wait()
    inside = (sec > 0) & (sec < sections - 1)

    @pl.when(inside)
    def _():
        pl.semaphore_wait(barrier, bits + 2)

    @pl.when(jnp.logical_not(inside))
    def _():
        pl.semaphore_wait(barrier, bits + 1)

    def exchange(b):
        copies = []
        for n in range(2):
            cols = slice(n * kvw, (n + 1) * kvw)
            copies.append(
                pltpu.make_async_remote_copy(
                    src_ref=p_v.at[:, cols] if b == 0 else kv_all.at[0:plen, cols],
                    dst_ref=kv_in.at[b, :, cols],
                    send_sem=x_send.at[b, n],
                    recv_sem=x_recv.at[b, n],
                    device_id={"resp": partners[b]},
                    device_id_type=MESH,
                )
            )
            copies[-1].start()
        return copies

    copies = exchange(0) if bits else None

    load_r.wait()
    load_q.wait()
    kv_all[plen : plen + near, :] = r_v[...]

    def turn_queries(i, unused):
        both = q_v[pl.ds(pl.multiple_of(i * 16, 16), 16), :].astype(F32)
        for half in range(2):
            part = both[half * CHUNK : (half + 1) * CHUNK, :]
            for p in range(pairs):
                heads = [
                    part[:, (p * 16 + j) * HEAD : (p * 16 + j + 1) * HEAD] for j in range(16)
                ]
                q_t[2 * i + half, p * HEAD : (p + 1) * HEAD, :] = jnp.concatenate(heads, 0)
        return unused

    lax.fori_loop(0, chunks // 2, turn_queries, 0)

    row = lax.broadcasted_iota(jnp.int32, (CHUNK, near), 0)
    key_row = lax.broadcasted_iota(jnp.int32, (CHUNK, near), 1)
    key_pos = key_row & (TOKM - 1)
    for micro in range(MB):
        key_resp = jnp.where(key_row - key_pos == micro * TOKM, 0, -1)
        ends = []
        for n in range(RESPS):
            ends.append((ends[-1] if n else 0) + seg[micro, n])
            key_resp = key_resp + jnp.where((key_pos >= ends[n]) & (key_resp >= 0), 1, 0)
        for part in range(TOKM // CHUNK):
            row_pos = row + part * CHUNK
            row_resp = jnp.zeros((CHUNK, near), jnp.int32)
            for end in ends:
                row_resp = row_resp + jnp.where(row_pos >= end, 1, 0)
            allowed = (key_resp == row_resp) & (key_pos <= row_pos)
            bias[micro * (TOKM // CHUNK) + part] = jnp.where(allowed, 0.0, -jnp.inf)

    root = lax.rem(owner[0, block], group)
    if not bits:
        kv_all[0:plen, :] = p_v[...]
    for b in range(bits):
        if b:
            copies = exchange(b)
        keep = lax.div(rank, 1 << b) == lax.div(root, 1 << b)
        for n in range(2):
            cols = slice(n * kvw, (n + 1) * kvw)
            copies[n].wait()
            held = p_v[:, cols] if b == 0 else kv_all[0:plen, cols]
            kv_all[0:plen, cols] = jnp.where(keep, held, kv_in[b, :, cols])

    factor = math.log2(math.e) / math.sqrt(HEAD)

    def forward(c):
        return pltpu.make_async_remote_copy(
            src_ref=sent.at[c],
            dst_ref=carry.at[c],
            send_sem=c_send.at[c],
            recv_sem=c_recv.at[c],
            device_id={"section": sec + 1},
            device_id_type=MESH,
        )

    def arrival(c):
        return pltpu.make_async_remote_copy(
            src_ref=sent.at[c],
            dst_ref=carry.at[c],
            send_sem=c_send.at[c],
            recv_sem=c_recv.at[c],
            device_id={"section": sec - 1},
            device_id_type=MESH,
        )

    def one_chunk(c):
        @pl.when(sec > 0)
        def _():
            arrival(c).wait_recv()

        attended = []
        square = jnp.zeros((CHUNK, HEAD), F32)
        masked = jnp.concatenate([bias[c]] * 16, 0)
        empty = jnp.zeros((HEAD // 2, HEAD), F32)
        middle = HEAD // 2
        for p in range(pairs):
            part = slice(p * HEAD, (p + 1) * HEAD)
            keys = slice(2 * p * HEAD, 2 * (p + 1) * HEAD)
            values = slice(kvw + 2 * p * HEAD, kvw + 2 * (p + 1) * HEAD)
            x = q_t[c, part, :] + carry[c, part, :].astype(F32)
            x = jnp.concatenate(
                [
                    jnp.concatenate([x[0:middle], empty], 1),
                    jnp.concatenate([empty, x[middle:]], 1),
                ],
                0,
            ).astype(BF16)
            over = (((1,), (1,)), ((), ()))
            far = lax.dot_general(x, kv_all[0:plen, keys], over, preferred_element_type=F32)
            close = lax.dot_general(x, kv_all[plen:, keys], over, preferred_element_type=F32)
            close = close + masked
            top = jnp.maximum(
                jnp.max(far, axis=1, keepdims=True), jnp.max(close, axis=1, keepdims=True)
            )
            far = jnp.exp2((far - top) * factor)
            close = jnp.exp2((close - top) * factor)
            total = jnp.sum(far, axis=1, keepdims=True) + jnp.sum(close, axis=1, keepdims=True)
            o = jnp.dot(far.astype(BF16), kv_all[0:plen, values], preferred_element_type=F32)
            o = o + jnp.dot(close.astype(BF16), kv_all[plen:, values], preferred_element_type=F32)
            o = jnp.concatenate([o[0:middle, 0:HEAD], o[middle:, HEAD:]], 0) * (1.0 / total)
            attended.append(o)
            for j in range(16):
                piece = o[j * CHUNK : (j + 1) * CHUNK]
                square = square + piece * piece
        norm = lax.rsqrt(jnp.sum(square, axis=1, keepdims=True) * (1.0 / wide) + EPS)
        norm = jnp.concatenate([jnp.broadcast_to(norm, (CHUNK, HEAD))] * 16, 0)
        for p in range(pairs):
            sent[c, p * HEAD : (p + 1) * HEAD, :] = (attended[p] * norm).astype(BF16)

        @pl.when(sec < sections - 1)
        def _():
            forward(c).start()

    def step(c, unused):
        one_chunk(c)
        return unused

    lax.fori_loop(0, chunks, step, 0)

    @pl.when(sec < sections - 1)
    def _():
        def finish(c, unused):
            forward(c).wait_send()
            return unused

        lax.fori_loop(0, chunks, finish, 0)


def turn_kernel(pairs, turned, out):
    for i in range(turned.shape[0] // 2):
        for p in range(pairs):
            part = slice(p * HEAD, (p + 1) * HEAD)
            first = turned[2 * i, part, :].astype(F32)
            second = turned[2 * i + 1, part, :].astype(F32)
            for j in range(16):
                rows = slice(j * CHUNK, (j + 1) * CHUNK)
                both = jnp.concatenate([first[rows], second[rows]], 0)
                column = (p * 16 + j) * HEAD
                out[0, 16 * i : 16 * (i + 1), column : column + HEAD] = both.astype(BF16)


def local(sections, bits, queries, resp_kv, prefix_kv, owner, seg_len):
    _, near, wide = queries.shape
    _, plen, kv2 = prefix_kv.shape
    kvw = kv2 // 2
    chunks = near // CHUNK
    pair_rows = kvw // 2
    steps = max(bits, 1)
    turned = pl.pallas_call(
        functools.partial(kernel, sections, bits),
        out_shape=jax.ShapeDtypeStruct((chunks, pair_rows, HEAD), BF16),
        in_specs=[pl.BlockSpec(memory_space=pl.ANY)] * 3
        + [pl.BlockSpec(memory_space=pltpu.SMEM)] * 2,
        out_specs=pl.BlockSpec(memory_space=pltpu.VMEM),
        scratch_shapes=[
            pltpu.VMEM((near, wide), BF16),
            pltpu.VMEM((near, kv2), BF16),
            pltpu.VMEM((plen, kv2), BF16),
            pltpu.VMEM((steps, plen, kv2), BF16),
            pltpu.VMEM((plen + near, kv2), BF16),
            pltpu.VMEM((chunks, pair_rows, HEAD), F32),
            pltpu.VMEM((chunks, pair_rows, HEAD), BF16),
            pltpu.VMEM((chunks, CHUNK, near), F32),
            pltpu.SemaphoreType.DMA((3,)),
            pltpu.SemaphoreType.DMA((steps, 2)),
            pltpu.SemaphoreType.DMA((steps, 2)),
            pltpu.SemaphoreType.DMA((chunks,)),
            pltpu.SemaphoreType.DMA((chunks,)),
        ],
        compiler_params=pltpu.CompilerParams(
            collective_id=0, has_side_effects=True, vmem_limit_bytes=60 * 1024 * 1024
        ),
        cost_estimate=pl.CostEstimate(
            flops=4 * near * wide * (plen + TOKM),
            bytes_accessed=4 * near * wide + 2 * (plen + near) * kv2,
            transcendentals=near * (wide // HEAD) * (plen + TOKM),
        ),
        name="layers",
    )(queries, resp_kv, prefix_kv, owner, seg_len)
    parts = 2
    return pl.pallas_call(
        functools.partial(turn_kernel, kvw // (2 * HEAD)),
        grid=(parts,),
        out_shape=jax.ShapeDtypeStruct(queries.shape, BF16),
        in_specs=[pl.BlockSpec((chunks // parts, pair_rows, HEAD), lambda i: (i, 0, 0))],
        out_specs=pl.BlockSpec((1, near // parts, wide), lambda i: (0, i, 0)),
        name="turn",
    )(turned)


def solution(mesh):
    sections = mesh.shape["section"]
    group = mesh.shape["resp"] // PROMPTS
    return jax.shard_map(
        functools.partial(local, sections, group.bit_length() - 1),
        mesh=mesh,
        in_specs=(
            P("section", "resp", None),
            P("section", "resp", None),
            P("section", "resp", None),
            P("section", None),
            P("resp", None),
        ),
        out_specs=P("section", "resp", None),
        check_vma=False,
    )
```
